32 devices in a mesh: wa: 8 (over z, x), ha: 4 (over y, core).
Axes of the slice: x: 2, y: 2, z: 4, core: 2. Of those that a mesh axis runs over, the one named last changes fastest.
Arguments:
- tokens: bfloat16 [256, 16384], P('ha', 'wa'), may hold values from -100 to 100, as said below
- norm_gain: float32 [16384], P('wa'), may hold values from 0.5 to 1.5
- gate_weight: bfloat16 [16384, 26624], P('wa', 'ha'), may hold values from -0.046875 to 0.046875
- up_weight: bfloat16 [16384, 26624], P('wa', 'ha'), may hold values from -0.046875 to 0.046875
- down_weight: bfloat16 [26624, 16384], P('ha', 'wa'), may hold values from -0.0390625 to 0.0390625
Outputs:
- mixed: bfloat16 [256, 16384], P('ha', 'wa')
The draws below stay inside these ranges and needn't reach their ends.
Inputs may be any that keep to these rules, and one draw needn't show every extreme that they name: `tokens`: real-valued activations.
All inputs are finite; a program needn't handle non-finite values.
Results may differ from the reference program's by a relative error of at most 0.0064.
Values may be sent and summed in bfloat16 or wider, within the bound.
No kernel may reach another device: no remote copies, remote signals or barrier semaphores. Data moves between devices by JAX's collectives and lax.ppermute only.
A program may use at most 192 MiB of HBM per device.

```python
import math
import jax
import jax.numpy as jnp
from jax import lax

D = 16384
FFW = 26624
TOKENS = 256


def draw_tokens(key, part):
    key_base, key_rows, key_columns = jax.random.split(key, 3)
    position = jnp.arange(D, dtype=jnp.float32)[None, :] / D
    row_scale = jnp.exp(jax.random.uniform(key_rows, (TOKENS, 1), jnp.float32, 0.0, math.log(10.0)))
    column_factor = jnp.exp(jax.random.uniform(key_columns, (1, D), jnp.float32, -0.6, 0.6))
    base = jnp.clip(jax.random.normal(key_base, (TOKENS, D), jnp.float32), -4.5, 4.5)
    rising = jnp.exp(position * math.log(3.0))
    return (0.3 * base * row_scale * column_factor * rising).astype(jnp.bfloat16)


def block_scale(rng, shape, cuts, low, largest):
    loudness, own = 1.0, jax.random.fold_in(rng, 6)
    for dim, shards_of in cuts:
        steps = jnp.exp(jax.random.uniform(jax.random.fold_in(own, dim), (shards_of,), jnp.float32, low / len(cuts), largest / len(cuts)))
        loudness = loudness * jnp.repeat(steps, shape[dim] // shards_of).reshape([-1 if axis == dim else 1 for axis in range(len(shape))])
    return loudness


def gaussian(rng, shape, scale, most, shards=(), kind=jnp.bfloat16):
    entries = jax.random.normal(rng, shape, jnp.float32) * scale
    if len(shards) > 0:
        entries = block_scale(rng, shape, shards, -0.22, 0.18) * entries
    return jnp.clip(entries, min=-most, max=most).astype(kind)


def setup_inputs(seed: int = 0) -> dict:
    key_list = jax.random.split(jax.random.key(seed), 6)
    return {
        "tokens": draw_tokens(jax.random.fold_in(key_list[5], 71), 0),
        "norm_gain": jnp.clip(1.0 + 0.1 * jax.random.normal(key_list[1], (D,), jnp.float32), 0.5, 1.5),
        "gate_weight": gaussian(key_list[2], (D, FFW), D ** -0.5, 0.046875, ((0, 8), (1, 4))),
        "up_weight": gaussian(key_list[3], (D, FFW), D ** -0.5, 0.046875, ((0, 8), (1, 4))),
        "down_weight": gaussian(key_list[4], (FFW, D), FFW ** -0.5, 0.0390625, ((0, 4), (1, 8))),
    }


def reference(tokens, norm_gain, gate_weight, up_weight, down_weight):
    values = tokens.astype(jnp.float32)
    squares = lax.optimization_barrier(jnp.mean(values * values, axis=1, keepdims=True))
    normed = (values * lax.rsqrt(squares + 1e-05) * norm_gain[None, :]).astype(jnp.bfloat16)
    gate = jnp.dot(normed, gate_weight, preferred_element_type=jnp.float32)
    up = jnp.dot(normed, up_weight, preferred_element_type=jnp.float32)
    hidden = (jax.nn.silu(gate) * up).astype(jnp.bfloat16)
    return jnp.dot(hidden, down_weight, preferred_element_type=jnp.float32).astype(jnp.bfloat16)
```

```python
import functools

import jax
import jax.numpy as jnp
from jax import lax
from jax.experimental import pallas as pl
from jax.experimental.pallas import tpu as pltpu
from jax.sharding import PartitionSpec as P

F32, BF16 = jnp.float32, jnp.bfloat16
EPS = 1e-05
VMEM_LIMIT = 48 * 1024 * 1024

X_SWAP = [(i, i ^ 1) for i in range(8)]
Z_SWAP = [(i, i ^ 2) for i in range(8)]
Z_CROSS = [(i, 6 - (i & 6) + (i & 1)) for i in range(8)]
Z_IN = [(0, 2), (1, 3), (6, 4), (7, 5)]
Z_OUT = [(2, 0), (3, 1), (4, 6), (5, 7)]
Z_MID = [(2, 4), (3, 5), (4, 2), (5, 3)]
X_MID = [(2, 3), (3, 2), (4, 5), (5, 4)]
Y_SWAP = [(i, i ^ 2) for i in range(4)]
CORE_SWAP = [(i, i ^ 1) for i in range(4)]


def any_spec():
    return pl.BlockSpec(memory_space=pl.ANY)


class Chain:
    def __init__(self):
        self.token = None

    def call(self, kernel, args, out_shape, *, grid=(), in_specs=None, out_specs=None, scratch=(), aliases=None, flops=1, name=None):
        args = list(args)
        if in_specs is None:
            in_specs = [pl.BlockSpec(memory_space=pltpu.VMEM)] * len(args)
        if out_specs is None:
            out_specs = [pl.BlockSpec(memory_space=pltpu.VMEM)] * len(out_shape)
        n_in = len(args)
        extra = 0
        if self.token is not None:
            args.append(self.token)
            in_specs = list(in_specs) + [any_spec()]
            extra = 1

        def run(*refs):
            kernel(*refs[:n_in], *refs[n_in + extra:])

        outs = pl.pallas_call(
            run,
            out_shape=tuple(out_shape),
            grid=grid,
            in_specs=in_specs,
            out_specs=tuple(out_specs),
            scratch_shapes=scratch,
            input_output_aliases=aliases or {},
            compiler_params=pltpu.CompilerParams(vmem_limit_bytes=VMEM_LIMIT),
            cost_estimate=pl.CostEstimate(flops=flops, bytes_accessed=1024, transcendentals=0),
            name=name,
        )(*args)
        self.token = outs[0]
        return outs


def shape(dims, dtype):
    return jax.ShapeDtypeStruct(tuple(dims), dtype)


def base_block():
    place = lax.axis_index("wa")
    return 2 * lax.rem(place, 2) + jnp.where(place >= 4, 1, 0)


def swap_bits(b):
    return 2 * lax.rem(b, 2) + b // 2


def xor(a, b):
    return lax.bitwise_xor(a, b)


def squares_kernel(t_ref, o_ref):
    v = t_ref[...].astype(F32)
    total = jnp.sum(v * v, axis=1, keepdims=True)
    o_ref[...] = jnp.broadcast_to(total, o_ref.shape)


def add_kernel(a_ref, b_ref, o_ref):
    o_ref[...] = a_ref[...] + b_ref[...]


def rows_at(position, rows):
    return pl.ds(pl.multiple_of(position * rows, rows), rows)


def arrange_kernel(t0, t2, t1, t3, g_ref, o_ref):
    rows = t0.shape[0]
    first = xor(lax.axis_index("ha"), base_block())
    for flip, t in ((0, t0), (2, t2), (1, t1), (3, t3)):
        o_ref[rows_at(xor(first, flip), rows), :] = (t[...].astype(F32) * g_ref[...]).astype(BF16)


def norm_kernel(width, t0, t2, t1, t3, s0, s2, s1, s3, g_ref, o_ref, r_ref):
    rows = t0.shape[0]
    first = xor(lax.axis_index("ha"), base_block())
    for flip, t, s in ((0, t0, s0), (2, t2, s2), (1, t1, s1), (3, t3, s3)):
        factor = lax.rsqrt(s[...] / width + EPS)
        at = rows_at(xor(first, flip), rows)
        o_ref[at, :] = (t[...].astype(F32) * factor[:, :1] * g_ref[...]).astype(BF16)
        r_ref[at, :] = factor


def project_kernel(lhs_ref, g_ref, u_ref, keep_ref, send_ref):
    half = lhs_ref.shape[0] // 2
    for i, w in enumerate((g_ref, u_ref)):
        total = jnp.dot(lhs_ref[...], w[...], preferred_element_type=F32)
        keep_ref[i] = total[:half]
        send_ref[i] = total[half:].astype(BF16)


def inward_kernel(keep_ref, x_ref, o_ref):
    o_ref[...] = (keep_ref[...] + x_ref[...].astype(F32)).astype(BF16)


def middle_kernel(keep_ref, x_ref, in_ref, o_ref):
    o_ref[...] = (keep_ref[...] + x_ref[...].astype(F32) + in_ref[...].astype(F32)).astype(BF16)


def activate_kernel(scaled, keep_ref, x_ref, in_ref, mid_ref, r_ref, o_ref):
    total = keep_ref[...] + x_ref[...].astype(F32) + in_ref[...].astype(F32) + mid_ref[...].astype(F32)
    if scaled:
        total = total * r_ref[...][None, :, :1]
    gate, up = total[0], total[1]
    o_ref[...] = (gate / (1.0 + jnp.exp(-gate)) * up).astype(BF16)


def join_kernel(a_ref, b_ref, o_ref):
    rows = a_ref.shape[0]
    o_ref[:rows, :] = a_ref[...]
    o_ref[rows:, :] = b_ref[...]


def pass_kernel(a_ref, o_ref):
    del a_ref, o_ref


def down_kernel(first, last, *refs):
    refs = list(refs)
    own_ref, mid_ref, out1_ref, out2_ref, w_ref = refs[:5]
    refs = refs[5:]
    if not first:
        acc_ref = refs.pop(0)
    hid_ref = refs[-1]
    half = own_ref.shape[0]

    @pl.when(pl.program_id(0) == 0)
    def _():
        place = lax.axis_index("wa")
        end = jnp.logical_or(place < 2, place >= 6)

        @pl.when(end)
        def _():
            hid_ref[:half, :] = out1_ref[...]
            hid_ref[half:, :] = out2_ref[...]

        @pl.when(jnp.logical_not(end))
        def _():
            hid_ref[:half, :] = own_ref[...]
            hid_ref[half:, :] = mid_ref[...]

    total = jnp.dot(hid_ref[...], w_ref[...], preferred_element_type=F32)
    if not first:
        total = total + acc_ref[...]
    if not last:
        refs[0][...] = total
        return
    keep_ref, send_ref, total_ref = refs[:3]
    total_ref[...] = total
    rows = half // 2
    here = xor(lax.axis_index("ha"), base_block())
    for flip, ref, at in ((0, keep_ref, 0), (2, keep_ref, 1), (1, send_ref, 0), (3, send_ref, 1)):
        part = total_ref[rows_at(swap_bits(xor(here, flip)), rows), :]
        ref[at * rows:(at + 1) * rows, :] = part.astype(ref.dtype)


def send_y_kernel(keep_ref, core_ref, o_ref):
    o_ref[...] = (keep_ref[...] + core_ref[...].astype(F32)).astype(BF16)


def final_kernel(keep_ref, core_ref, y_ref, o_ref):
    o_ref[...] = (keep_ref[...] + core_ref[...].astype(F32) + y_ref[...].astype(F32)).astype(BF16)


def chunk_units(units):
    shares = (5, 5, 5, 4, 4, 3)
    total, done, cuts = sum(shares), 0, [0]
    for s in shares:
        done += s
        cuts.append(units * done // total)
    return cuts


def planned(tokens, norm_gain, gate_weight, up_weight, down_weight):
    rows, width = tokens.shape
    hidden = gate_weight.shape[1]
    out_width = down_weight.shape[1]
    tile = 256
    cuts = [c * tile for c in chunk_units(hidden // tile)]
    n_chunks = len(cuts) - 1
    gain = norm_gain[None, :]
    chain = Chain()
    swap = lambda a, axis, pairs: lax.ppermute(a, axis, pairs)

    (sq,) = chain.call(squares_kernel, [tokens], [shape((rows, 128), F32)], name="squares")
    t2 = swap(tokens, "ha", Y_SWAP)
    t1 = swap(tokens, "ha", CORE_SWAP)
    t3 = swap(t2, "ha", CORE_SWAP)
    for pairs in (X_SWAP, Z_SWAP):
        (sq,) = chain.call(add_kernel, [sq, swap(sq, "wa", pairs)], [shape((rows, 128), F32)], name="squares_add")
    sq_cross = swap(sq, "wa", Z_CROSS)
    (lhs_raw,) = chain.call(arrange_kernel, [tokens, t2, t1, t3, gain], [shape((4 * rows, width), BF16)], name="arrange")

    def project(k, lhs):
        n = cuts[k + 1] - cuts[k]
        first = cuts[k] // tile
        return chain.call(
            project_kernel,
            [lhs, gate_weight, up_weight],
            [shape((2, 2 * rows, n), F32), shape((2, 2 * rows, n), BF16)],
            grid=(n // tile,),
            in_specs=[
                pl.BlockSpec((4 * rows, width), lambda i: (0, 0)),
                pl.BlockSpec((width, tile), lambda i: (0, first + i)),
                pl.BlockSpec((width, tile), lambda i: (0, first + i)),
            ],
            out_specs=[pl.BlockSpec((2, 2 * rows, tile), lambda i: (0, 0, i))] * 2,
            name="project",
        )

    state = [dict() for _ in range(n_chunks)]
    env = {"acc": None, "lhs": None, "r": None, "sq": sq, "sq_cross": sq_cross}

    def stage_q(k):
        (s0,) = chain.call(add_kernel, [env["sq"], env["sq_cross"]], [shape((rows, 128), F32)], name="squares_add")
        s2 = swap(s0, "ha", Y_SWAP)
        s1 = swap(s0, "ha", CORE_SWAP)
        s3 = swap(s2, "ha", CORE_SWAP)
        env["s"] = (s0, s2, s1, s3)

    def stage_n(k):
        env["lhs"], env["r"] = chain.call(
            functools.partial(norm_kernel, width * lax.axis_size("wa")),
            [tokens, t2, t1, t3, *env["s"], gain],
            [shape((4 * rows, width), BF16), shape((4 * rows, 128), F32)],
            name="norm",
        )

    def stage_m(k):
        s = state[k]
        s["scaled"] = env["lhs"] is None
        s["keep"], send = project(k, lhs_raw if s["scaled"] else env["lhs"])
        s["x"] = swap(send, "wa", X_SWAP)

    def part(n, at):
        return pl.BlockSpec((2, rows, n), lambda i: (0, at, 0))

    def width_of(k):
        return cuts[k + 1] - cuts[k]

    def stage_i(k):
        s = state[k]
        n = width_of(k)
        (send,) = chain.call(inward_kernel, [s["keep"], s["x"]], [shape((2, 2 * rows, n), BF16)], name="inward")
        s["in"] = swap(send, "wa", Z_IN)

    def stage_j(k):
        s = state[k]
        n = width_of(k)
        (send,) = chain.call(
            middle_kernel, [s["keep"], s["x"], s["in"]], [shape((2, rows, n), BF16)],
            grid=(1,), in_specs=[part(n, 1)] * 3, out_specs=[part(n, 0)], name="middle",
        )
        s["mid"] = swap(send, "wa", Z_MID)

    def stage_h(k):
        s = state[k]
        n = width_of(k)
        r = env["r"]
        (s["h"],) = chain.call(
            functools.partial(activate_kernel, s["scaled"]),
            [s["keep"], s["x"], s["in"], s["mid"], r],
            [shape((rows, n), BF16)],
            grid=(1,),
            in_specs=[part(n, 0)] * 4 + [pl.BlockSpec((rows, 128), lambda i: (0, 0))],
            out_specs=[pl.BlockSpec((rows, n), lambda i: (0, 0))],
            name="activate",
        )
        s["hx"] = swap(s["h"], "wa", X_MID)

    def stage_g(k):
        s = state[k]
        n = width_of(k)
        (s["own"],) = chain.call(join_kernel, [s["h"], s["hx"]], [shape((2 * rows, n), BF16)], name="join")
        s["hm"] = swap(s["own"], "wa", Z_MID)
        s["o1"] = swap(s["own"], "wa", Z_OUT)

    def stage_r(k):
        s = state[k]
        n = width_of(k)
        (s["hm"],) = chain.call(
            pass_kernel, [s["hm"]], [shape((2 * rows, n), BF16)],
            in_specs=[any_spec()], out_specs=[any_spec()], aliases={0: 0}, name="pass",
        )
        s["o2"] = swap(s["hm"], "wa", Z_OUT)

    def stage_w(k):
        s = state[k]
        n = width_of(k)
        first, last = k == 0, k == n_chunks - 1
        cols = 512
        whole = pl.BlockSpec((2 * rows, n), lambda i: (0, 0))
        args = [s["own"], s["hm"], s["o1"], s["o2"], lax.slice(down_weight, (cuts[k], 0), (cuts[k + 1], out_width))]
        args[4] = down_weight
        at = cuts[k]
        in_specs = [whole] * 4 + [pl.BlockSpec((pl.Element(n), pl.Element(cols)), lambda i: (at, i * cols))]
        if not first:
            args.append(env["acc"])
            in_specs.append(pl.BlockSpec((4 * rows, cols), lambda i: (0, i)))
        if last:
            out_shape = [shape((2 * rows, out_width), F32), shape((2 * rows, out_width), BF16)]
            out_specs = [pl.BlockSpec((2 * rows, cols), lambda i: (0, i))] * 2
            scratch = [pltpu.VMEM((4 * rows, cols), F32), pltpu.VMEM((4 * rows, n), BF16)]
        else:
            out_shape = [shape((4 * rows, out_width), F32)]
            out_specs = [pl.BlockSpec((4 * rows, cols), lambda i: (0, i))]
            scratch = [pltpu.VMEM((4 * rows, n), BF16)]
        outs = chain.call(
            functools.partial(down_kernel, first, last), args, out_shape,
            grid=(out_width // cols,), in_specs=in_specs, out_specs=out_specs, scratch=scratch, name="down",
        )
        env["acc"] = outs[0]
        env["last"] = outs

    stages = dict(m=stage_m, i=stage_i, j=stage_j, h=stage_h, g=stage_g, r=stage_r, w=stage_w, q=stage_q, n=stage_n)
    for step in ORDER:
        stages[step[0]](int(step[1:] or 0))

    keep, send = env["last"]
    core = swap(send, "ha", CORE_SWAP)
    block = lambda at: pl.BlockSpec((rows, out_width), lambda i: (at, 0))
    (send_y,) = chain.call(
        send_y_kernel, [keep, core], [shape((rows, out_width), BF16)],
        grid=(1,), in_specs=[block(1), block(1)], out_specs=[block(0)], name="send_y",
    )
    y = swap(send_y, "ha", Y_SWAP)
    (out,) = chain.call(
        final_kernel, [keep, core, y], [shape((rows, out_width), BF16)],
        grid=(1,), in_specs=[block(0)] * 3, out_specs=[block(0)], name="final",
    )
    return out


ORDER = (
    "m0", "q", "m1", "n", "i0", "m2", "j0", "i1", "h0", "m3", "g0", "j1",
    "i2", "r0", "h1", "m4", "g1", "j2", "w0", "i3", "r1", "h2", "m5", "g2",
    "j3", "w1", "i4", "r2", "h3", "g3", "j4", "w2", "i5", "r3", "h4", "g4",
    "j5", "w3", "r4", "h5", "g5", "w4", "r5", "w5",
)


def general(tokens, norm_gain, gate_weight, up_weight, down_weight):
    gathered = lax.all_gather(tokens, "ha", axis=0, tiled=True).astype(F32)
    squares = lax.psum(jnp.sum(gathered * gathered, axis=1), "wa")
    mean_square = squares[:, None] / (gathered.shape[1] * lax.axis_size("wa"))
    normed = (gathered * lax.rsqrt(mean_square + EPS) * norm_gain[None, :]).astype(BF16)
    hidden = gate_weight.shape[1]
    gate = jnp.dot(normed, gate_weight, preferred_element_type=F32)
    up = jnp.dot(normed, up_weight, preferred_element_type=F32)
    summed = lax.psum_scatter(jnp.concatenate([gate, up], axis=1), "wa", scatter_dimension=0, tiled=True)
    mixed = (jax.nn.silu(summed[:, :hidden]) * summed[:, hidden:]).astype(BF16)
    out = jnp.dot(lax.all_gather(mixed, "wa", axis=0, tiled=True), down_weight, preferred_element_type=F32)
    return lax.psum_scatter(out, "ha", scatter_dimension=0, tiled=True).astype(BF16)


def solution(mesh):
    body = planned if (mesh.shape["wa"], mesh.shape["ha"]) == (8, 4) else general
    placed = (P("ha", "wa"), P("wa"), P("wa", "ha"), P("wa", "ha"), P("ha", "wa"))
    return jax.shard_map(body, mesh=mesh, in_specs=placed, out_specs=P("ha", "wa"), check_vma=False)
```

```python
import functools

import jax
import jax.numpy as jnp
from jax import lax
from jax.experimental import pallas as pl
from jax.experimental.pallas import tpu as pltpu
from jax.sharding import PartitionSpec as P

F32, BF16 = jnp.float32, jnp.bfloat16
EPS = 1e-05
VMEM_LIMIT = 48 * 1024 * 1024

AXES = ("wa", "ha")
X, Z_LOW, Z_HIGH = 1, 2, 4


def swaps(wa_flips=(0, 0), ha_flip=0):
    return [(w * 4 + h, (w ^ wa_flips[h % 2]) * 4 + (h ^ ha_flip)) for w in range(8) for h in range(4)]


FIRST = swaps((X, Z_LOW))
SECOND = swaps((Z_LOW, X))
THIRD = swaps((Z_HIGH, Z_HIGH))
CORE_SWAP = swaps(ha_flip=1)
Y_SWAP = swaps(ha_flip=2)


def swap(a, pairs):
    return lax.ppermute(a, AXES, pairs)


def any_spec():
    return pl.BlockSpec(memory_space=pl.ANY)


class Chain:
    def __init__(self):
        self.token = None

    def call(self, kernel, args, out_shape, *, grid=(), in_specs=None, out_specs=None, scratch=(), aliases=None, flops=1, name=None):
        args = list(args)
        if in_specs is None:
            in_specs = [pl.BlockSpec(memory_space=pltpu.VMEM)] * len(args)
        if out_specs is None:
            out_specs = [pl.BlockSpec(memory_space=pltpu.VMEM)] * len(out_shape)
        n_in = len(args)
        extra = 0
        if self.token is not None:
            args.append(self.token)
            in_specs = list(in_specs) + [any_spec()]
            extra = 1

        def run(*refs):
            kernel(*refs[:n_in], *refs[n_in + extra:])

        outs = pl.pallas_call(
            run,
            out_shape=tuple(out_shape),
            grid=grid,
            in_specs=in_specs,
            out_specs=tuple(out_specs),
            scratch_shapes=scratch,
            input_output_aliases=aliases or {},
            compiler_params=pltpu.CompilerParams(vmem_limit_bytes=VMEM_LIMIT),
            cost_estimate=pl.CostEstimate(flops=flops, bytes_accessed=1024, transcendentals=0),
            name=name,
        )(*args)
        self.token = outs[0]
        return outs


def shape(dims, dtype):
    return jax.ShapeDtypeStruct(tuple(dims), dtype)


def own_block():
    place, core = lax.axis_index("wa"), lax.rem(lax.axis_index("ha"), 2)
    x, low, high = lax.rem(place, 2), lax.rem(place // 2, 2), place // 4
    return jnp.where(core == 0, 4 * x + 2 * low, 4 * low + 2 * x) + high


def token_rows(flip, part, rows):
    block = 2 * lax.bitwise_xor(lax.axis_index("ha"), flip) + part
    return pl.ds(pl.multiple_of(lax.bitwise_xor(block, own_block()) * rows, rows), rows)


def squares_kernel(t_ref, o_ref):
    v = t_ref[...].astype(F32)
    total = jnp.sum(v * v, axis=1, keepdims=True)
    o_ref[...] = jnp.broadcast_to(total, o_ref.shape)


def add_kernel(a_ref, b_ref, o_ref):
    o_ref[...] = a_ref[...] + b_ref[...]


def arrange_kernel(t0, t1, t2, t3, g_ref, o_ref):
    half = t0.shape[0] // 2
    for flip, t in enumerate((t0, t1, t2, t3)):
        v = (t[...].astype(F32) * g_ref[...]).astype(BF16)
        for part in range(2):
            o_ref[token_rows(flip, part, half), :] = v[part * half:(part + 1) * half]


def norm_kernel(width, t0, t1, t2, t3, s0, s1, s2, s3, g_ref, o_ref, r_ref):
    half = t0.shape[0] // 2
    for flip, (t, s) in enumerate(((t0, s0), (t1, s1), (t2, s2), (t3, s3))):
        factor = lax.rsqrt(s[...] / width + EPS)
        v = (t[...].astype(F32) * factor[:, :1] * g_ref[...]).astype(BF16)
        for part in range(2):
            at = token_rows(flip, part, half)
            o_ref[at, :] = v[part * half:(part + 1) * half]
            r_ref[at, :] = factor[part * half:(part + 1) * half]


def project_kernel(lhs_ref, g_ref, u_ref, keep_ref, send_ref):
    half = lhs_ref.shape[0] // 2
    for i, w in enumerate((g_ref, u_ref)):
        total = jnp.dot(lhs_ref[...], w[...], preferred_element_type=F32)
        keep_ref[i] = total[:half]
        send_ref[i] = total[half:].astype(BF16)


def sum_of(keep_ref, parts):
    total = keep_ref[...]
    for p in parts:
        total = total + p[...].astype(F32)
    return total


def add_up_kernel(keep_ref, *refs):
    refs[-1][...] = sum_of(keep_ref, refs[:-1]).astype(BF16)


def activate_kernel(scaled, keep_ref, p1_ref, p2_ref, p3_ref, r_ref, o_ref):
    total = sum_of(keep_ref, (p1_ref, p2_ref, p3_ref))
    if scaled:
        total = total * r_ref[...][None, :, :1]
    gate, up = total[0], total[1]
    o_ref[...] = (gate / (1.0 + jnp.exp(-gate)) * up).astype(BF16)


def join_kernel(a_ref, b_ref, o_ref):
    rows = a_ref.shape[0]
    o_ref[:rows, :] = a_ref[...]
    o_ref[rows:, :] = b_ref[...]


def pass_kernel(a_ref, o_ref):
    del a_ref, o_ref


def down_kernel(n_parts, first, last, *refs):
    refs = list(refs)
    parts, w_ref, refs = refs[:2 * n_parts], refs[2 * n_parts], refs[2 * n_parts + 1:]
    if not first:
        acc_ref = refs.pop(0)
    hid_ref = refs[-1]
    half = hid_ref.shape[0] // 2

    @pl.when(pl.program_id(0) == 0)
    def _():
        at = 0
        for i in range(n_parts):
            own, other = parts[2 * i:2 * i + 2]
            n = own.shape[1]
            hid_ref[:half, at:at + n] = own[...]
            hid_ref[half:, at:at + n] = other[...]
            at += n

    total = jnp.dot(hid_ref[...], w_ref[...], preferred_element_type=F32)
    if not first:
        total = total + acc_ref[...]
    if not last:
        refs[0][...] = total
        return
    keep_ref, send_ref, total_ref = refs[:3]
    total_ref[...] = total
    rows = half // 4
    for flip, ref, at in ((0, keep_ref, 0), (2, keep_ref, 2), (1, send_ref, 0), (3, send_ref, 2)):
        for part in range(2):
            v = total_ref[token_rows(flip, part, rows), :]
            ref[(at + part) * rows:(at + part + 1) * rows, :] = v.astype(ref.dtype)


def send_y_kernel(keep_ref, core_ref, o_ref):
    o_ref[...] = (keep_ref[...] + core_ref[...].astype(F32)).astype(BF16)


def final_kernel(keep_ref, core_ref, y_ref, o_ref):
    o_ref[...] = (keep_ref[...] + core_ref[...].astype(F32) + y_ref[...].astype(F32)).astype(BF16)


SHARES = (6, 4, 4, 6, 6)
GROUPS = ((0,), (1,), (2,), (3,), (4,),)
ORDER = (
    "q", "m0", "n", "m1", "a0", "m2", "a1", "m3", "b0", "a2", "b1", "m4",
    "a3", "c0", "b2", "c1", "a4", "b3", "d0", "c2", "d1", "b4", "c3", "e0",
    "d2", "e1", "c4", "d3", "e2", "w0", "d4", "e3", "w1", "e4", "w2", "w3",
    "w4",
)


def planned(tokens, norm_gain, gate_weight, up_weight, down_weight):
    rows, width = tokens.shape
    hidden = gate_weight.shape[1]
    out_width = down_weight.shape[1]
    unit = hidden // sum(SHARES)
    cuts = [unit * sum(SHARES[:k]) for k in range(len(SHARES) + 1)]
    gain = norm_gain[None, :]
    chain = Chain()

    t0 = tokens
    sq_shape = shape((rows, 128), F32)
    (sq,) = chain.call(squares_kernel, [t0], [sq_shape], name="squares")
    t2 = swap(t0, Y_SWAP)
    t1 = swap(t0, CORE_SWAP)
    (sq,) = chain.call(add_kernel, [sq, swap(sq, FIRST)], [sq_shape], name="squares_add")
    sq_second = swap(sq, SECOND)
    (t2,) = chain.call(
        pass_kernel, [t2], [shape(t2.shape, BF16)], in_specs=[any_spec()], out_specs=[any_spec()], aliases={0: 0}, name="pass",
    )
    t3 = swap(t2, CORE_SWAP)
    (sq,) = chain.call(add_kernel, [sq, sq_second], [sq_shape], name="squares_add")
    sq_third = swap(sq, THIRD)
    (raw,) = chain.call(arrange_kernel, [t0, t1, t2, t3, gain], [shape((4 * rows, width), BF16)], name="arrange")

    state = [dict() for _ in SHARES]
    env = {"lhs": raw, "acc": None}

    def stage_q(k):
        (s0,) = chain.call(add_kernel, [sq, sq_third], [sq_shape], name="squares_add")
        s2 = swap(s0, Y_SWAP)
        s1 = swap(s0, CORE_SWAP)
        env["s"] = (s0, s1, s2, swap(s2, CORE_SWAP))

    def stage_n(k):
        env["lhs"], env["r"] = chain.call(
            functools.partial(norm_kernel, width * lax.axis_size("wa")),
            [t0, t1, t2, t3, *env["s"], gain],
            [shape((4 * rows, width), BF16), shape((4 * rows, 128), F32)],
            name="norm",
        )

    def stage_m(k):
        s = state[k]
        n = s["n"] = cuts[k + 1] - cuts[k]
        s["scaled"] = "r" not in env
        tile = 512 if n % 512 == 0 and cuts[k] % 512 == 0 else 256
        first = cuts[k] // tile
        s["keep"], send = chain.call(
            project_kernel,
            [env["lhs"], gate_weight, up_weight],
            [shape((2, 2 * rows, n), F32), shape((2, 2 * rows, n), BF16)],
            grid=(n // tile,),
            in_specs=[
                pl.BlockSpec((4 * rows, width), lambda i: (0, 0)),
                pl.BlockSpec((width, tile), lambda i: (0, first + i)),
                pl.BlockSpec((width, tile), lambda i: (0, first + i)),
            ],
            out_specs=[pl.BlockSpec((2, 2 * rows, tile), lambda i: (0, 0, i))] * 2,
            name="project",
        )
        s["parts"] = [swap(send, FIRST)]

    def part(n, size, at):
        return pl.BlockSpec((2, size, n), lambda i: (0, at, 0))

    def add_up(k, size, pairs):
        s = state[k]
        n = s["n"]
        (send,) = chain.call(
            add_up_kernel, [s["keep"], *s["parts"]], [shape((2, size, n), BF16)],
            grid=(1,), in_specs=[part(n, size, 1)] * (1 + len(s["parts"])), out_specs=[part(n, size, 0)], name="add_up",
        )
        s["parts"].append(swap(send, pairs))

    def stage_a(k):
        add_up(k, rows, SECOND)

    def stage_b(k):
        add_up(k, rows // 2, THIRD)

    def stage_c(k):
        s = state[k]
        n, size = s["n"], rows // 2
        (s["h"],) = chain.call(
            functools.partial(activate_kernel, s["scaled"]),
            [s["keep"], *s["parts"], env["r"]],
            [shape((size, n), BF16)],
            grid=(1,),
            in_specs=[part(n, size, 0)] * 4 + [pl.BlockSpec((size, 128), lambda i: (0, 0))],
            out_specs=[pl.BlockSpec((size, n), lambda i: (0, 0))],
            name="activate",
        )
        s["got"] = swap(s["h"], THIRD)

    def join(k, pairs):
        s = state[k]
        (s["h"],) = chain.call(
            join_kernel, [s["h"], s["got"]], [shape((2 * s["h"].shape[0], s["n"]), BF16)], name="join"
        )
        s["got"] = swap(s["h"], pairs)

    def stage_d(k):
        join(k, SECOND)

    def stage_e(k):
        join(k, FIRST)

    def stage_w(k):
        group = GROUPS[k]
        first, last = k == 0, k == len(GROUPS) - 1
        at, n = cuts[group[0]], cuts[group[-1] + 1] - cuts[group[0]]
        cols = 512
        args, in_specs = [], []
        for j in group:
            args += [state[j]["h"], state[j]["got"]]
            in_specs += [pl.BlockSpec((2 * rows, state[j]["n"]), lambda i: (0, 0))] * 2
        args.append(down_weight)
        in_specs.append(pl.BlockSpec((pl.Element(n), pl.Element(cols)), lambda i: (at, i * cols)))
        if not first:
            args.append(env["acc"])
            in_specs.append(pl.BlockSpec((4 * rows, cols), lambda i: (0, i)))
        if last:
            out_shape = [shape((2 * rows, out_width), F32), shape((2 * rows, out_width), BF16)]
            out_specs = [pl.BlockSpec((2 * rows, cols), lambda i: (0, i))] * 2
            scratch = [pltpu.VMEM((4 * rows, cols), F32), pltpu.VMEM((4 * rows, n), BF16)]
        else:
            out_shape = [shape((4 * rows, out_width), F32)]
            out_specs = [pl.BlockSpec((4 * rows, cols), lambda i: (0, i))]
            scratch = [pltpu.VMEM((4 * rows, n), BF16)]
        env["last"] = chain.call(
            functools.partial(down_kernel, len(group), first, last), args, out_shape,
            grid=(out_width // cols,), in_specs=in_specs, out_specs=out_specs, scratch=scratch, name="down",
        )
        env["acc"] = env["last"][0]

    stages = dict(
        m=stage_m, a=stage_a, b=stage_b, c=stage_c, d=stage_d, e=stage_e, w=stage_w, q=stage_q, n=stage_n
    )
    for step in ORDER:
        stages[step[0]](int(step[1:] or 0))

    keep, send = env["last"]
    core = swap(send, CORE_SWAP)
    block = lambda at: pl.BlockSpec((rows, out_width), lambda i: (at, 0))
    (send_y,) = chain.call(
        send_y_kernel, [keep, core], [shape((rows, out_width), BF16)],
        grid=(1,), in_specs=[block(1), block(1)], out_specs=[block(0)], name="send_y",
    )
    y = swap(send_y, Y_SWAP)
    (out,) = chain.call(
        final_kernel, [keep, core, y], [shape((rows, out_width), BF16)],
        grid=(1,), in_specs=[block(0)] * 3, out_specs=[block(0)], name="final",
    )
    return out


def general(tokens, norm_gain, gate_weight, up_weight, down_weight):
    gathered = lax.all_gather(tokens, "ha", axis=0, tiled=True).astype(F32)
    squares = lax.psum(jnp.sum(gathered * gathered, axis=1), "wa")
    mean_square = squares[:, None] / (gathered.shape[1] * lax.axis_size("wa"))
    normed = (gathered * lax.rsqrt(mean_square + EPS) * norm_gain[None, :]).astype(BF16)
    hidden = gate_weight.shape[1]
    gate = jnp.dot(normed, gate_weight, preferred_element_type=F32)
    up = jnp.dot(normed, up_weight, preferred_element_type=F32)
    summed = lax.psum_scatter(jnp.concatenate([gate, up], axis=1), "wa", scatter_dimension=0, tiled=True)
    mixed = (jax.nn.silu(summed[:, :hidden]) * summed[:, hidden:]).astype(BF16)
    out = jnp.dot(lax.all_gather(mixed, "wa", axis=0, tiled=True), down_weight, preferred_element_type=F32)
    return lax.psum_scatter(out, "ha", scatter_dimension=0, tiled=True).astype(BF16)


def solution(mesh):
    body = planned if (mesh.shape["wa"], mesh.shape["ha"]) == (8, 4) else general
    placed = (P("ha", "wa"), P("wa"), P("wa", "ha"), P("wa", "ha"), P("ha", "wa"))
    return jax.shard_map(body, mesh=mesh, in_specs=placed, out_specs=P("ha", "wa"), check_vma=False)
```

```python
import functools

import jax
import jax.numpy as jnp
from jax import lax
from jax.experimental import pallas as pl
from jax.experimental.pallas import tpu as pltpu
from jax.sharding import PartitionSpec as P

F32, BF16 = jnp.float32, jnp.bfloat16
EPS = 1e-05
SMALL_FLOPS, UNIT_FLOPS = 4 * 10**9, 25 * 10**7
VMEM_LIMIT = 48 * 1024 * 1024

AXES = ("wa", "ha")
X, Z_LOW, Z_HIGH = 1, 2, 4


def swaps(wa_flips=(0, 0), ha_flip=0):
    return [(w * 4 + h, (w ^ wa_flips[h % 2]) * 4 + (h ^ ha_flip)) for w in range(8) for h in range(4)]


MODES = {"m": (X, Z_LOW), "n": (Z_LOW, X), "x": (X, X), "z": (Z_LOW, Z_LOW)}
FIRST = {mode: swaps(bits) for mode, bits in MODES.items()}
SECOND = {mode: swaps([X + Z_LOW - b for b in bits]) for mode, bits in MODES.items()}
THIRD = swaps((Z_HIGH, Z_HIGH))
CORE_SWAP = swaps(ha_flip=1)
Y_SWAP = swaps(ha_flip=2)


def swap(a, pairs):
    return lax.ppermute(a, AXES, pairs)


def any_spec():
    return pl.BlockSpec(memory_space=pl.ANY)


class Chain:
    def __init__(self):
        self.token = None

    def call(self, kernel, args, out_shape, *, grid=(), in_specs=None, out_specs=None, scratch=(), aliases=None, flops=SMALL_FLOPS, name=None):
        args = list(args)
        if in_specs is None:
            in_specs = [pl.BlockSpec(memory_space=pltpu.VMEM)] * len(args)
        if out_specs is None:
            out_specs = [pl.BlockSpec(memory_space=pltpu.VMEM)] * len(out_shape)
        n_in = len(args)
        extra = 0
        if self.token is not None:
            args.append(self.token)
            in_specs = list(in_specs) + [any_spec()]
            extra = 1

        def run(*refs):
            kernel(*refs[:n_in], *refs[n_in + extra:])

        outs = pl.pallas_call(
            run,
            out_shape=tuple(out_shape),
            grid=grid,
            in_specs=in_specs,
            out_specs=tuple(out_specs),
            scratch_shapes=scratch,
            input_output_aliases=aliases or {},
            compiler_params=pltpu.CompilerParams(vmem_limit_bytes=VMEM_LIMIT),
            cost_estimate=pl.CostEstimate(flops=flops, bytes_accessed=1024, transcendentals=0),
            name=name,
        )(*args)
        self.token = outs[0]
        return outs


def shape(dims, dtype):
    return jax.ShapeDtypeStruct(tuple(dims), dtype)


def own_block():
    place, core = lax.axis_index("wa"), lax.rem(lax.axis_index("ha"), 2)
    x, low, high = lax.rem(place, 2), lax.rem(place // 2, 2), place // 4
    return jnp.where(core == 0, 4 * x + 2 * low, 4 * low + 2 * x) + high


def token_rows(flip, part, rows):
    block = 2 * lax.bitwise_xor(lax.axis_index("ha"), flip) + part
    return pl.ds(pl.multiple_of(lax.bitwise_xor(block, own_block()) * rows, rows), rows)


def squares_kernel(t_ref, o_ref):
    v = t_ref[...].astype(F32)
    total = jnp.sum(v * v, axis=1, keepdims=True)
    o_ref[...] = jnp.broadcast_to(total, o_ref.shape)


def add_kernel(a_ref, b_ref, o_ref):
    o_ref[...] = a_ref[...] + b_ref[...]


def arrange_kernel(t0, t1, t2, t3, g_ref, o_ref):
    half = t0.shape[0] // 2
    for flip, t in enumerate((t0, t1, t2, t3)):
        v = (t[...].astype(F32) * g_ref[...]).astype(BF16)
        for part in range(2):
            o_ref[token_rows(flip, part, half), :] = v[part * half:(part + 1) * half]


def norm_kernel(width, t0, t1, t2, t3, s0, s1, s2, s3, g_ref, o_ref, r_ref):
    half = t0.shape[0] // 2
    for flip, (t, s) in enumerate(((t0, s0), (t1, s1), (t2, s2), (t3, s3))):
        factor = lax.rsqrt(s[...] / width + EPS)
        v = (t[...].astype(F32) * factor[:, :1] * g_ref[...]).astype(BF16)
        for part in range(2):
            at = token_rows(flip, part, half)
            o_ref[at, :] = v[part * half:(part + 1) * half]
            r_ref[at, :] = factor[part * half:(part + 1) * half]


def crossed(mode, a, b):
    differs = [p != q for p, q in zip(MODES[mode], MODES["m"])]
    if all(differs):
        return b, a
    if not any(differs):
        return a, b
    swapped = lax.rem(lax.axis_index("ha"), 2) == differs.index(True)
    return jnp.where(swapped, b, a), jnp.where(swapped, a, b)


def project_kernel(mode, lhs_ref, g_ref, u_ref, keep_ref, send_ref):
    quarter = lhs_ref.shape[0] // 4
    half = 2 * quarter
    for i, w in enumerate((g_ref, u_ref)):
        total = jnp.dot(lhs_ref[...], w[...], preferred_element_type=F32)
        second, third = crossed(mode, total[quarter:half], total[half:half + quarter])
        keep_ref[i, :quarter] = total[:quarter]
        keep_ref[i, quarter:] = second
        send_ref[i, :quarter] = third.astype(BF16)
        send_ref[i, quarter:] = total[half + quarter:].astype(BF16)


def sum_of(keep_ref, parts):
    total = keep_ref[...]
    for p in parts:
        total = total + p[...].astype(F32)
    return total


def add_up_kernel(keep_ref, *refs):
    refs[-1][...] = sum_of(keep_ref, refs[:-1]).astype(BF16)


def activate_kernel(scaled, keep_ref, p1_ref, p2_ref, p3_ref, r_ref, o_ref):
    total = sum_of(keep_ref, (p1_ref, p2_ref, p3_ref))
    if scaled:
        total = total * r_ref[...][None, :, :1]
    gate, up = total[0], total[1]
    o_ref[...] = (gate / (1.0 + jnp.exp(-gate)) * up).astype(BF16)


def join_kernel(a_ref, b_ref, o_ref):
    rows = a_ref.shape[0]
    o_ref[:rows, :] = a_ref[...]
    o_ref[rows:, :] = b_ref[...]


def pass_kernel(a_ref, o_ref):
    del a_ref, o_ref


def down_kernel(modes, first, last, *refs):
    refs, n_parts = list(refs), len(modes)
    parts, w_ref, refs = refs[:2 * n_parts], refs[2 * n_parts], refs[2 * n_parts + 1:]
    if not first:
        acc_ref = refs.pop(0)
    hid_ref = refs[-1]
    half = hid_ref.shape[0] // 2

    @pl.when(pl.program_id(0) == 0)
    def _():
        at = 0
        for i in range(n_parts):
            own, other = parts[2 * i:2 * i + 2]
            n = own.shape[1]
            quarter = half // 2
            second, third = crossed(modes[i], own[quarter:], other[:quarter])
            hid_ref[:quarter, at:at + n] = own[:quarter]
            hid_ref[quarter:half, at:at + n] = second
            hid_ref[half:half + quarter, at:at + n] = third
            hid_ref[half + quarter:, at:at + n] = other[quarter:]
            at += n

    total = jnp.dot(hid_ref[...], w_ref[...], preferred_element_type=F32)
    if not first:
        total = total + acc_ref[...]
    if not last:
        refs[0][...] = total
        return
    keep_ref, send_ref, total_ref = refs[:3]
    total_ref[...] = total
    rows = half // 4
    for flip, ref, at in ((0, keep_ref, 0), (2, keep_ref, 2), (1, send_ref, 0), (3, send_ref, 2)):
        for part in range(2):
            v = total_ref[token_rows(flip, part, rows), :]
            ref[(at + part) * rows:(at + part + 1) * rows, :] = v.astype(ref.dtype)


def send_y_kernel(keep_ref, core_ref, o_ref):
    o_ref[...] = (keep_ref[...] + core_ref[...].astype(F32)).astype(BF16)


def final_kernel(keep_ref, core_ref, y_ref, o_ref):
    o_ref[...] = (keep_ref[...] + core_ref[...].astype(F32) + y_ref[...].astype(F32)).astype(BF16)


SHARES = (6, 6, 8, 6,)
SUM, GATHER = "mmmm", "nnnn"
GROUPS = ((0, 1,), (2,), (3,),)
ORDER = (
    "m0", "s", "m1", "a0", "q", "n", "m2", "b0", "a1", "m3", "c0", "b1",
    "a2", "d0", "c1", "b2", "a3", "e0", "d1", "c2", "b3", "e1", "d2", "c3",
    "w0", "e2", "d3", "e3", "w1", "w2",
)


def planned(tokens, norm_gain, gate_weight, up_weight, down_weight):
    rows, width = tokens.shape
    hidden = gate_weight.shape[1]
    out_width = down_weight.shape[1]
    unit = hidden // sum(SHARES)
    cuts = [unit * sum(SHARES[:k]) for k in range(len(SHARES) + 1)]
    gain = norm_gain[None, :]
    chain = Chain()

    t0 = tokens
    sq_shape = shape((rows, 128), F32)
    t2 = swap(t0, Y_SWAP)
    t1 = swap(t0, CORE_SWAP)
    (sq,) = chain.call(squares_kernel, [t0], [sq_shape], name="squares")
    squares = [sq, swap(sq, FIRST["m"])]
    (t2,) = chain.call(
        pass_kernel, [t2], [shape(t2.shape, BF16)], in_specs=[any_spec()], out_specs=[any_spec()], aliases={0: 0}, name="pass",
    )
    t3 = swap(t2, CORE_SWAP)
    (sq,) = chain.call(add_kernel, squares, [sq_shape], name="squares_add")
    squares = [sq, swap(sq, SECOND["m"])]
    (raw,) = chain.call(arrange_kernel, [t0, t1, t2, t3, gain], [shape((4 * rows, width), BF16)], name="arrange")

    state = [dict() for _ in SHARES]
    env = {"lhs": raw, "acc": None}

    def stage_s(k):
        (total,) = chain.call(add_kernel, squares, [sq_shape], name="squares_add")
        squares[:] = total, swap(total, THIRD)

    def stage_q(k):
        (s0,) = chain.call(add_kernel, squares, [sq_shape], name="squares_add")
        s2 = swap(s0, Y_SWAP)
        s1 = swap(s0, CORE_SWAP)
        env["s"] = (s0, s1, s2, swap(s2, CORE_SWAP))

    def stage_n(k):
        env["lhs"], env["r"] = chain.call(
            functools.partial(norm_kernel, width * lax.axis_size("wa")),
            [t0, t1, t2, t3, *env["s"], gain],
            [shape((4 * rows, width), BF16), shape((4 * rows, 128), F32)],
            name="norm",
        )

    def stage_m(k):
        s = state[k]
        n = s["n"] = cuts[k + 1] - cuts[k]
        s["scaled"] = "r" not in env
        tile = 512 if n % 512 == 0 and cuts[k] % 512 == 0 else 256
        first = cuts[k] // tile
        s["keep"], send = chain.call(
            functools.partial(project_kernel, SUM[k]),
            [env["lhs"], gate_weight, up_weight],
            [shape((2, 2 * rows, n), F32), shape((2, 2 * rows, n), BF16)],
            grid=(n // tile,),
            in_specs=[
                pl.BlockSpec((4 * rows, width), lambda i: (0, 0)),
                pl.BlockSpec((width, tile), lambda i: (0, first + i)),
                pl.BlockSpec((width, tile), lambda i: (0, first + i)),
            ],
            out_specs=[pl.BlockSpec((2, 2 * rows, tile), lambda i: (0, 0, i))] * 2,
            flops=UNIT_FLOPS * 5 * SHARES[k],
            name="project",
        )
        s["parts"] = [swap(send, FIRST[SUM[k]])]

    def part(n, size, at):
        return pl.BlockSpec((2, size, n), lambda i: (0, at, 0))

    def add_up(k, size, pairs):
        s = state[k]
        n = s["n"]
        (send,) = chain.call(
            add_up_kernel, [s["keep"], *s["parts"]], [shape((2, size, n), BF16)],
            grid=(1,), in_specs=[part(n, size, 1)] * (1 + len(s["parts"])), out_specs=[part(n, size, 0)], name="add_up",
        )
        s["parts"].append(swap(send, pairs))

    def stage_a(k):
        add_up(k, rows, SECOND[SUM[k]])

    def stage_b(k):
        add_up(k, rows // 2, THIRD)

    def stage_c(k):
        s = state[k]
        n, size = s["n"], rows // 2
        (s["h"],) = chain.call(
            functools.partial(activate_kernel, s["scaled"]),
            [s["keep"], *s["parts"], env["r"]],
            [shape((size, n), BF16)],
            grid=(1,),
            in_specs=[part(n, size, 0)] * 4 + [pl.BlockSpec((size, 128), lambda i: (0, 0))],
            out_specs=[pl.BlockSpec((size, n), lambda i: (0, 0))],
            name="activate",
        )
        s["got"] = swap(s["h"], THIRD)

    def join(k, pairs):
        s = state[k]
        (s["h"],) = chain.call(
            join_kernel, [s["h"], s["got"]], [shape((2 * s["h"].shape[0], s["n"]), BF16)], name="join"
        )
        s["got"] = swap(s["h"], pairs)

    def stage_d(k):
        join(k, SECOND[GATHER[k]])

    def stage_e(k):
        join(k, FIRST[GATHER[k]])

    def stage_w(k):
        group = GROUPS[k]
        first, last = k == 0, k == len(GROUPS) - 1
        at, n = cuts[group[0]], cuts[group[-1] + 1] - cuts[group[0]]
        cols = 512
        args, in_specs = [], []
        for j in group:
            args += [state[j]["h"], state[j]["got"]]
            in_specs += [pl.BlockSpec((2 * rows, state[j]["n"]), lambda i: (0, 0))] * 2
        args.append(down_weight)
        in_specs.append(pl.BlockSpec((pl.Element(n), pl.Element(cols)), lambda i: (at, i * cols)))
        if not first:
            args.append(env["acc"])
            in_specs.append(pl.BlockSpec((4 * rows, cols), lambda i: (0, i)))
        if last:
            out_shape = [shape((2 * rows, out_width), F32), shape((2 * rows, out_width), BF16)]
            out_specs = [pl.BlockSpec((2 * rows, cols), lambda i: (0, i))] * 2
            scratch = [pltpu.VMEM((4 * rows, cols), F32), pltpu.VMEM((4 * rows, n), BF16)]
        else:
            out_shape = [shape((4 * rows, out_width), F32)]
            out_specs = [pl.BlockSpec((4 * rows, cols), lambda i: (0, i))]
            scratch = [pltpu.VMEM((4 * rows, n), BF16)]
        env["last"] = chain.call(
            functools.partial(down_kernel, [GATHER[j] for j in group], first, last), args, out_shape,
            grid=(out_width // cols,), in_specs=in_specs, out_specs=out_specs, scratch=scratch,
            flops=UNIT_FLOPS * 2 * sum(SHARES[j] for j in group), name="down",
        )
        env["acc"] = env["last"][0]

    stages = dict(
        m=stage_m, a=stage_a, b=stage_b, c=stage_c, d=stage_d, e=stage_e, w=stage_w, s=stage_s, q=stage_q, n=stage_n
    )
    for step in ORDER:
        stages[step[0]](int(step[1:] or 0))

    keep, send = env["last"]
    core = swap(send, CORE_SWAP)
    block = lambda at: pl.BlockSpec((rows, out_width), lambda i: (at, 0))
    (send_y,) = chain.call(
        send_y_kernel, [keep, core], [shape((rows, out_width), BF16)],
        grid=(1,), in_specs=[block(1), block(1)], out_specs=[block(0)], name="send_y",
    )
    y = swap(send_y, Y_SWAP)
    (out,) = chain.call(
        final_kernel, [keep, core, y], [shape((rows, out_width), BF16)],
        grid=(1,), in_specs=[block(0)] * 3, out_specs=[block(0)], name="final",
    )
    return out


def general(tokens, norm_gain, gate_weight, up_weight, down_weight):
    gathered = lax.all_gather(tokens, "ha", axis=0, tiled=True).astype(F32)
    squares = lax.psum(jnp.sum(gathered * gathered, axis=1), "wa")
    mean_square = squares[:, None] / (gathered.shape[1] * lax.axis_size("wa"))
    normed = (gathered * lax.rsqrt(mean_square + EPS) * norm_gain[None, :]).astype(BF16)
    hidden = gate_weight.shape[1]
    gate = jnp.dot(normed, gate_weight, preferred_element_type=F32)
    up = jnp.dot(normed, up_weight, preferred_element_type=F32)
    summed = lax.psum_scatter(jnp.concatenate([gate, up], axis=1), "wa", scatter_dimension=0, tiled=True)
    mixed = (jax.nn.silu(summed[:, :hidden]) * summed[:, hidden:]).astype(BF16)
    out = jnp.dot(lax.all_gather(mixed, "wa", axis=0, tiled=True), down_weight, preferred_element_type=F32)
    return lax.psum_scatter(out, "ha", scatter_dimension=0, tiled=True).astype(BF16)


def solution(mesh):
    body = planned if (mesh.shape["wa"], mesh.shape["ha"]) == (8, 4) else general
    placed = (P("ha", "wa"), P("wa"), P("wa", "ha"), P("wa", "ha"), P("ha", "wa"))
    return jax.shard_map(body, mesh=mesh, in_specs=placed, out_specs=P("ha", "wa"), check_vma=False)
```

```python
import functools

import jax
import jax.numpy as jnp
from jax import lax
from jax.experimental import pallas as pl
from jax.experimental.pallas import tpu as pltpu
from jax.sharding import PartitionSpec as P

F32, BF16 = jnp.float32, jnp.bfloat16
EPS = 1e-05
SMALL_FLOPS, UNIT_FLOPS = 4 * 10**9, 25 * 10**7
VMEM_LIMIT = 48 * 1024 * 1024

AXES = ("wa", "ha")
X, Z_LOW, Z_HIGH = 1, 2, 4


def swaps(wa_flips=(0, 0), ha_flip=0):
    return [(w * 4 + h, (w ^ wa_flips[h % 2]) * 4 + (h ^ ha_flip)) for w in range(8) for h in range(4)]


MODES = {"m": (X, Z_LOW), "n": (Z_LOW, X), "x": (X, X), "z": (Z_LOW, Z_LOW)}
FIRST = {mode: swaps(bits) for mode, bits in MODES.items()}
SECOND = {mode: swaps([X + Z_LOW - b for b in bits]) for mode, bits in MODES.items()}
THIRD = swaps((Z_HIGH, Z_HIGH))
CORE_SWAP = swaps(ha_flip=1)
Y_SWAP = swaps(ha_flip=2)
BOTH_SWAP = swaps(ha_flip=3)


def swap(a, pairs):
    return lax.ppermute(a, AXES, pairs)


def any_spec():
    return pl.BlockSpec(memory_space=pl.ANY)


class Chain:
    def __init__(self):
        self.token = None

    def call(self, kernel, args, out_shape, *, grid=(), in_specs=None, out_specs=None, scratch=(), aliases=None, flops=SMALL_FLOPS, name=None):
        args = list(args)
        if in_specs is None:
            in_specs = [pl.BlockSpec(memory_space=pltpu.VMEM)] * len(args)
        if out_specs is None:
            out_specs = [pl.BlockSpec(memory_space=pltpu.VMEM)] * len(out_shape)
        n_in = len(args)
        extra = 0
        if self.token is not None:
            args.append(self.token)
            in_specs = list(in_specs) + [any_spec()]
            extra = 1

        def run(*refs):
            kernel(*refs[:n_in], *refs[n_in + extra:])

        outs = pl.pallas_call(
            run,
            out_shape=tuple(out_shape),
            grid=grid,
            in_specs=in_specs,
            out_specs=tuple(out_specs),
            scratch_shapes=scratch,
            input_output_aliases=aliases or {},
            compiler_params=pltpu.CompilerParams(vmem_limit_bytes=VMEM_LIMIT),
            cost_estimate=pl.CostEstimate(flops=flops, bytes_accessed=1024, transcendentals=0),
            name=name,
        )(*args)
        self.token = outs[0]
        return outs


def shape(dims, dtype):
    return jax.ShapeDtypeStruct(tuple(dims), dtype)


def own_block():
    place, core = lax.axis_index("wa"), lax.rem(lax.axis_index("ha"), 2)
    x, low, high = lax.rem(place, 2), lax.rem(place // 2, 2), place // 4
    return jnp.where(core == 0, 4 * x + 2 * low, 4 * low + 2 * x) + high


def token_rows(flip, part, rows):
    block = 2 * lax.bitwise_xor(lax.axis_index("ha"), flip) + part
    return pl.ds(pl.multiple_of(lax.bitwise_xor(block, own_block()) * rows, rows), rows)


def squares_kernel(t_ref, o_ref):
    v = t_ref[...].astype(F32)
    total = jnp.sum(v * v, axis=1, keepdims=True)
    o_ref[...] = jnp.broadcast_to(total, o_ref.shape)


def add_kernel(a_ref, b_ref, o_ref):
    o_ref[...] = a_ref[...] + b_ref[...]


def arrange_kernel(t0, t1, t2, t3, g_ref, o_ref):
    half = t0.shape[0] // 2
    for flip, t in enumerate((t0, t1, t2, t3)):
        v = (t[...].astype(F32) * g_ref[...]).astype(BF16)
        for part in range(2):
            o_ref[token_rows(flip, part, half), :] = v[part * half:(part + 1) * half]


def norm_kernel(width, t0, t1, t2, t3, s0, s1, s2, s3, g_ref, o_ref, r_ref):
    half = t0.shape[0] // 2
    for flip, (t, s) in enumerate(((t0, s0), (t1, s1), (t2, s2), (t3, s3))):
        factor = lax.rsqrt(s[...] / width + EPS)
        v = (t[...].astype(F32) * factor[:, :1] * g_ref[...]).astype(BF16)
        for part in range(2):
            at = token_rows(flip, part, half)
            o_ref[at, :] = v[part * half:(part + 1) * half]
            r_ref[at, :] = factor[part * half:(part + 1) * half]


def crossed(mode, a, b):
    differs = [p != q for p, q in zip(MODES[mode], MODES["m"])]
    if all(differs):
        return b, a
    if not any(differs):
        return a, b
    swapped = lax.rem(lax.axis_index("ha"), 2) == differs.index(True)
    return jnp.where(swapped, b, a), jnp.where(swapped, a, b)


def project_kernel(mode, lhs_ref, g_ref, u_ref, keep_ref, send_ref):
    quarter = lhs_ref.shape[0] // 4
    half = 2 * quarter
    for i, w in enumerate((g_ref, u_ref)):
        total = jnp.dot(lhs_ref[...], w[...], preferred_element_type=F32)
        second, third = crossed(mode, total[quarter:half], total[half:half + quarter])
        keep_ref[i, :quarter] = total[:quarter]
        keep_ref[i, quarter:] = second
        send_ref[i, :quarter] = third.astype(BF16)
        send_ref[i, quarter:] = total[half + quarter:].astype(BF16)


def sum_of(keep_ref, parts):
    total = keep_ref[...]
    for p in parts:
        total = total + p[...].astype(F32)
    return total


def add_up_kernel(keep_ref, *refs):
    refs[-1][...] = sum_of(keep_ref, refs[:-1]).astype(BF16)


def activate_kernel(scaled, keep_ref, p1_ref, p2_ref, p3_ref, r_ref, o_ref):
    total = sum_of(keep_ref, (p1_ref, p2_ref, p3_ref))
    if scaled:
        total = total * r_ref[...][None, :, :1]
    gate, up = total[0], total[1]
    o_ref[...] = (gate / (1.0 + jnp.exp(-gate)) * up).astype(BF16)


def join_kernel(a_ref, b_ref, o_ref):
    rows = a_ref.shape[0]
    o_ref[:rows, :] = a_ref[...]
    o_ref[rows:, :] = b_ref[...]


def pass_kernel(a_ref, o_ref):
    del a_ref, o_ref


def down_kernel(modes, first, last, *refs):
    refs, n_parts = list(refs), len(modes)
    parts, w_ref, refs = refs[:2 * n_parts], refs[2 * n_parts], refs[2 * n_parts + 1:]
    if not first:
        acc_ref = refs.pop(0)
    hid_ref = refs[-1]
    half = hid_ref.shape[0] // 2

    @pl.when(pl.program_id(0) == 0)
    def _():
        at = 0
        for i in range(n_parts):
            own, other = parts[2 * i:2 * i + 2]
            n = own.shape[1]
            quarter = half // 2
            second, third = crossed(modes[i], own[quarter:], other[:quarter])
            hid_ref[:quarter, at:at + n] = own[:quarter]
            hid_ref[quarter:half, at:at + n] = second
            hid_ref[half:half + quarter, at:at + n] = third
            hid_ref[half + quarter:, at:at + n] = other[quarter:]
            at += n

    total = jnp.dot(hid_ref[...], w_ref[...], preferred_element_type=F32)
    if not first:
        total = total + acc_ref[...]
    if not last:
        refs[0][...] = total
        return
    keep_ref, send_ref, total_ref = refs[:3]
    total_ref[...] = total
    rows = half // 4
    for flip, ref, at in ((0, keep_ref, 0), (2, keep_ref, 2), (1, send_ref, 0), (3, send_ref, 2)):
        for part in range(2):
            v = total_ref[token_rows(flip, part, rows), :]
            ref[(at + part) * rows:(at + part + 1) * rows, :] = v.astype(ref.dtype)


def send_y_kernel(keep_ref, core_ref, o_ref):
    o_ref[...] = (keep_ref[...] + core_ref[...].astype(F32)).astype(BF16)


def final_kernel(keep_ref, core_ref, y_ref, o_ref):
    o_ref[...] = (keep_ref[...] + core_ref[...].astype(F32) + y_ref[...].astype(F32)).astype(BF16)


SHARES = (6, 6, 8, 6,)
SUM, GATHER = "mmmm", "nnmm"
GROUPS = ((0, 1,), (2,), (3,),)
ORDER = (
    "m0", "s", "m1", "a0", "q", "n", "m2", "b0", "a1", "m3", "c0", "b1",
    "a2", "d0", "c1", "b2", "a3", "e0", "d1", "c2", "b3", "e1", "d2", "c3",
    "w0", "e2", "d3", "e3", "w1", "w2",
)


def planned(tokens, norm_gain, gate_weight, up_weight, down_weight):
    rows, width = tokens.shape
    hidden = gate_weight.shape[1]
    out_width = down_weight.shape[1]
    unit = hidden // sum(SHARES)
    cuts = [unit * sum(SHARES[:k]) for k in range(len(SHARES) + 1)]
    gain = norm_gain[None, :]
    chain = Chain()

    t0 = tokens
    sq_shape = shape((rows, 128), F32)
    t2 = swap(t0, Y_SWAP)
    t1 = swap(t0, CORE_SWAP)
    (sq,) = chain.call(squares_kernel, [t0], [sq_shape], name="squares")
    squares = [sq, swap(sq, FIRST["m"])]
    (t2,) = chain.call(
        pass_kernel, [t2], [shape(t2.shape, BF16)], in_specs=[any_spec()], out_specs=[any_spec()], aliases={0: 0}, name="pass",
    )
    t3 = swap(t2, CORE_SWAP)
    (sq,) = chain.call(add_kernel, squares, [sq_shape], name="squares_add")
    squares = [sq, swap(sq, SECOND["m"])]
    (raw,) = chain.call(arrange_kernel, [t0, t1, t2, t3, gain], [shape((4 * rows, width), BF16)], name="arrange")

    state = [dict() for _ in SHARES]
    env = {"lhs": raw, "acc": None}

    def stage_s(k):
        (total,) = chain.call(add_kernel, squares, [sq_shape], name="squares_add")
        squares[:] = total, swap(total, THIRD)

    def stage_q(k):
        (s0,) = chain.call(add_kernel, squares, [sq_shape], name="squares_add")
        s2 = swap(s0, Y_SWAP)
        s1 = swap(s0, CORE_SWAP)
        env["s"] = (s0, s1, s2, swap(s0, BOTH_SWAP))

    def stage_n(k):
        env["lhs"], env["r"] = chain.call(
            functools.partial(norm_kernel, width * lax.axis_size("wa")),
            [t0, t1, t2, t3, *env["s"], gain],
            [shape((4 * rows, width), BF16), shape((4 * rows, 128), F32)],
            name="norm",
        )

    def stage_m(k):
        s = state[k]
        n = s["n"] = cuts[k + 1] - cuts[k]
        s["scaled"] = "r" not in env
        tile = 512 if n % 512 == 0 and cuts[k] % 512 == 0 else 256
        first = cuts[k] // tile
        s["keep"], send = chain.call(
            functools.partial(project_kernel, SUM[k]),
            [env["lhs"], gate_weight, up_weight],
            [shape((2, 2 * rows, n), F32), shape((2, 2 * rows, n), BF16)],
            grid=(n // tile,),
            in_specs=[
                pl.BlockSpec((4 * rows, width), lambda i: (0, 0)),
                pl.BlockSpec((width, tile), lambda i: (0, first + i)),
                pl.BlockSpec((width, tile), lambda i: (0, first + i)),
            ],
            out_specs=[pl.BlockSpec((2, 2 * rows, tile), lambda i: (0, 0, i))] * 2,
            flops=UNIT_FLOPS * 5 * SHARES[k],
            name="project",
        )
        s["parts"] = [swap(send, FIRST[SUM[k]])]

    def part(n, size, at):
        return pl.BlockSpec((2, size, n), lambda i: (0, at, 0))

    def add_up(k, size, pairs):
        s = state[k]
        n = s["n"]
        (send,) = chain.call(
            add_up_kernel, [s["keep"], *s["parts"]], [shape((2, size, n), BF16)],
            grid=(1,), in_specs=[part(n, size, 1)] * (1 + len(s["parts"])), out_specs=[part(n, size, 0)], name="add_up",
        )
        s["parts"].append(swap(send, pairs))

    def stage_a(k):
        add_up(k, rows, SECOND[SUM[k]])

    def stage_b(k):
        add_up(k, rows // 2, THIRD)

    def stage_c(k):
        s = state[k]
        n, size = s["n"], rows // 2
        (s["h"],) = chain.call(
            functools.partial(activate_kernel, s["scaled"]),
            [s["keep"], *s["parts"], env["r"]],
            [shape((size, n), BF16)],
            grid=(1,),
            in_specs=[part(n, size, 0)] * 4 + [pl.BlockSpec((size, 128), lambda i: (0, 0))],
            out_specs=[pl.BlockSpec((size, n), lambda i: (0, 0))],
            name="activate",
        )
        s["got"] = swap(s["h"], THIRD)

    def join(k, pairs):
        s = state[k]
        (s["h"],) = chain.call(
            join_kernel, [s["h"], s["got"]], [shape((2 * s["h"].shape[0], s["n"]), BF16)], name="join"
        )
        s["got"] = swap(s["h"], pairs)

    def stage_d(k):
        join(k, SECOND[GATHER[k]])

    def stage_e(k):
        join(k, FIRST[GATHER[k]])

    def stage_w(k):
        group = GROUPS[k]
        first, last = k == 0, k == len(GROUPS) - 1
        at, n = cuts[group[0]], cuts[group[-1] + 1] - cuts[group[0]]
        cols = 1024
        args, in_specs = [], []
        for j in group:
            args += [state[j]["h"], state[j]["got"]]
            in_specs += [pl.BlockSpec((2 * rows, state[j]["n"]), lambda i: (0, 0))] * 2
        args.append(down_weight)
        in_specs.append(pl.BlockSpec((pl.Element(n), pl.Element(cols)), lambda i: (at, i * cols)))
        if not first:
            args.append(env["acc"])
            in_specs.append(pl.BlockSpec((4 * rows, cols), lambda i: (0, i)))
        if last:
            out_shape = [shape((2 * rows, out_width), F32), shape((2 * rows, out_width), BF16)]
            out_specs = [pl.BlockSpec((2 * rows, cols), lambda i: (0, i))] * 2
            scratch = [pltpu.VMEM((4 * rows, cols), F32), pltpu.VMEM((4 * rows, n), BF16)]
        else:
            out_shape = [shape((4 * rows, out_width), F32)]
            out_specs = [pl.BlockSpec((4 * rows, cols), lambda i: (0, i))]
            scratch = [pltpu.VMEM((4 * rows, n), BF16)]
        env["last"] = chain.call(
            functools.partial(down_kernel, [GATHER[j] for j in group], first, last), args, out_shape,
            grid=(out_width // cols,), in_specs=in_specs, out_specs=out_specs, scratch=scratch,
            flops=UNIT_FLOPS * 2 * sum(SHARES[j] for j in group), name="down",
        )
        env["acc"] = env["last"][0]

    stages = dict(
        m=stage_m, a=stage_a, b=stage_b, c=stage_c, d=stage_d, e=stage_e, w=stage_w, s=stage_s, q=stage_q, n=stage_n
    )
    for step in ORDER:
        stages[step[0]](int(step[1:] or 0))

    keep, send = env["last"]
    core = swap(send, CORE_SWAP)
    block = lambda at: pl.BlockSpec((rows, out_width), lambda i: (at, 0))
    (send_y,) = chain.call(
        send_y_kernel, [keep, core], [shape((rows, out_width), BF16)],
        grid=(1,), in_specs=[block(1), block(1)], out_specs=[block(0)], name="send_y",
    )
    y = swap(send_y, Y_SWAP)
    (out,) = chain.call(
        final_kernel, [keep, core, y], [shape((rows, out_width), BF16)],
        grid=(1,), in_specs=[block(0)] * 3, out_specs=[block(0)], name="final",
    )
    return out


def general(tokens, norm_gain, gate_weight, up_weight, down_weight):
    gathered = lax.all_gather(tokens, "ha", axis=0, tiled=True).astype(F32)
    squares = lax.psum(jnp.sum(gathered * gathered, axis=1), "wa")
    mean_square = squares[:, None] / (gathered.shape[1] * lax.axis_size("wa"))
    normed = (gathered * lax.rsqrt(mean_square + EPS) * norm_gain[None, :]).astype(BF16)
    hidden = gate_weight.shape[1]
    gate = jnp.dot(normed, gate_weight, preferred_element_type=F32)
    up = jnp.dot(normed, up_weight, preferred_element_type=F32)
    summed = lax.psum_scatter(jnp.concatenate([gate, up], axis=1), "wa", scatter_dimension=0, tiled=True)
    mixed = (jax.nn.silu(summed[:, :hidden]) * summed[:, hidden:]).astype(BF16)
    out = jnp.dot(lax.all_gather(mixed, "wa", axis=0, tiled=True), down_weight, preferred_element_type=F32)
    return lax.psum_scatter(out, "ha", scatter_dimension=0, tiled=True).astype(BF16)


def solution(mesh):
    body = planned if (mesh.shape["wa"], mesh.shape["ha"]) == (8, 4) else general
    placed = (P("ha", "wa"), P("wa"), P("wa", "ha"), P("wa", "ha"), P("ha", "wa"))
    return jax.shard_map(body, mesh=mesh, in_specs=placed, out_specs=P("ha", "wa"), check_vma=False)
```

```python
import functools

import jax
import jax.numpy as jnp
from jax import lax
from jax.experimental import pallas as pl
from jax.experimental.pallas import tpu as pltpu
from jax.sharding import PartitionSpec as P

F32, BF16 = jnp.float32, jnp.bfloat16
EPS = 1e-05
SMALL_FLOPS, UNIT_FLOPS = 4 * 10**9, 25 * 10**7
VMEM_LIMIT = 48 * 1024 * 1024

AXES = ("wa", "ha")
X, Z_LOW, Z_HIGH = 1, 2, 4


def swaps(wa_flips=(0, 0), ha_flip=0):
    return [(w * 4 + h, (w ^ wa_flips[h % 2]) * 4 + (h ^ ha_flip)) for w in range(8) for h in range(4)]


MODES = {"m": (X, Z_LOW), "n": (Z_LOW, X), "x": (X, X), "z": (Z_LOW, Z_LOW)}
FIRST = {mode: swaps(bits) for mode, bits in MODES.items()}
SECOND = {mode: swaps([X + Z_LOW - b for b in bits]) for mode, bits in MODES.items()}
THIRD = swaps((Z_HIGH, Z_HIGH))
CORE_SWAP = swaps(ha_flip=1)
Y_SWAP = swaps(ha_flip=2)
BOTH_SWAP = swaps(ha_flip=3)


def swap(a, pairs):
    return lax.ppermute(a, AXES, pairs)


def any_spec():
    return pl.BlockSpec(memory_space=pl.ANY)


class Chain:
    def __init__(self):
        self.token = None

    def call(self, kernel, args, out_shape, *, grid=(), in_specs=None, out_specs=None, scratch=(), aliases=None, flops=SMALL_FLOPS, name=None):
        args = list(args)
        if in_specs is None:
            in_specs = [pl.BlockSpec(memory_space=pltpu.VMEM)] * len(args)
        if out_specs is None:
            out_specs = [pl.BlockSpec(memory_space=pltpu.VMEM)] * len(out_shape)
        n_in = len(args)
        extra = 0
        if self.token is not None:
            args.append(self.token)
            in_specs = list(in_specs) + [any_spec()]
            extra = 1

        def run(*refs):
            kernel(*refs[:n_in], *refs[n_in + extra:])

        outs = pl.pallas_call(
            run,
            out_shape=tuple(out_shape),
            grid=grid,
            in_specs=in_specs,
            out_specs=tuple(out_specs),
            scratch_shapes=scratch,
            input_output_aliases=aliases or {},
            compiler_params=pltpu.CompilerParams(vmem_limit_bytes=VMEM_LIMIT),
            cost_estimate=pl.CostEstimate(flops=flops, bytes_accessed=1024, transcendentals=0),
            name=name,
        )(*args)
        self.token = outs[0]
        return outs


def shape(dims, dtype):
    return jax.ShapeDtypeStruct(tuple(dims), dtype)


def own_block():
    place, core = lax.axis_index("wa"), lax.rem(lax.axis_index("ha"), 2)
    x, low, high = lax.rem(place, 2), lax.rem(place // 2, 2), place // 4
    return jnp.where(core == 0, 4 * x + 2 * low, 4 * low + 2 * x) + high


def token_rows(flip, part, rows):
    block = 2 * lax.bitwise_xor(lax.axis_index("ha"), flip) + part
    return pl.ds(pl.multiple_of(lax.bitwise_xor(block, own_block()) * rows, rows), rows)


def squares_kernel(t_ref, o_ref):
    v = t_ref[...].astype(F32)
    total = jnp.sum(v * v, axis=1, keepdims=True)
    o_ref[...] = jnp.broadcast_to(total, o_ref.shape)


def add_kernel(a_ref, b_ref, o_ref):
    o_ref[...] = a_ref[...] + b_ref[...]


def arrange_kernel(t0, t1, t2, t3, g_ref, o_ref):
    half = t0.shape[0] // 2
    for flip, t in enumerate((t0, t1, t2, t3)):
        v = (t[...].astype(F32) * g_ref[...]).astype(BF16)
        for part in range(2):
            o_ref[token_rows(flip, part, half), :] = v[part * half:(part + 1) * half]


def norm_kernel(width, t0, t1, t2, t3, s0, s1, s2, s3, g_ref, o_ref, r_ref):
    half = t0.shape[0] // 2
    for flip, (t, s) in enumerate(((t0, s0), (t1, s1), (t2, s2), (t3, s3))):
        factor = lax.rsqrt(s[...] / width + EPS)
        v = (t[...].astype(F32) * factor[:, :1] * g_ref[...]).astype(BF16)
        for part in range(2):
            at = token_rows(flip, part, half)
            o_ref[at, :] = v[part * half:(part + 1) * half]
            r_ref[at, :] = factor[part * half:(part + 1) * half]


def crossed(mode, a, b):
    differs = [p != q for p, q in zip(MODES[mode], MODES["m"])]
    if all(differs):
        return b, a
    if not any(differs):
        return a, b
    swapped = lax.rem(lax.axis_index("ha"), 2) == differs.index(True)
    return jnp.where(swapped, b, a), jnp.where(swapped, a, b)


def project_kernel(mode, lhs_ref, g_ref, u_ref, keep_ref, send_ref):
    quarter = lhs_ref.shape[0] // 4
    half = 2 * quarter
    for i, w in enumerate((g_ref, u_ref)):
        total = jnp.dot(lhs_ref[...], w[...], preferred_element_type=F32)
        second, third = crossed(mode, total[quarter:half], total[half:half + quarter])
        keep_ref[i, :quarter] = total[:quarter]
        keep_ref[i, quarter:] = second
        send_ref[i, :quarter] = third.astype(BF16)
        send_ref[i, quarter:] = total[half + quarter:].astype(BF16)


def sum_of(keep_ref, parts):
    total = keep_ref[...]
    for p in parts:
        total = total + p[...].astype(F32)
    return total


def add_up_kernel(keep_ref, *refs):
    refs[-1][...] = sum_of(keep_ref, refs[:-1]).astype(BF16)


def activate_kernel(scaled, keep_ref, p1_ref, p2_ref, p3_ref, r_ref, o_ref):
    total = sum_of(keep_ref, (p1_ref, p2_ref, p3_ref))
    if scaled:
        total = total * r_ref[...][None, :, :1]
    gate, up = total[0], total[1]
    o_ref[...] = (gate / (1.0 + jnp.exp(-gate)) * up).astype(BF16)


def join_kernel(a_ref, b_ref, o_ref):
    rows = a_ref.shape[0]
    o_ref[:rows, :] = a_ref[...]
    o_ref[rows:, :] = b_ref[...]


def pass_kernel(a_ref, o_ref):
    del a_ref, o_ref


def down_kernel(modes, first, last, *refs):
    refs, n_parts = list(refs), len(modes)
    parts, w_ref, refs = refs[:2 * n_parts], refs[2 * n_parts], refs[2 * n_parts + 1:]
    if not first:
        acc_ref = refs.pop(0)
    hid_ref = refs[-1]
    half = hid_ref.shape[0] // 2

    @pl.when(pl.program_id(0) == 0)
    def _():
        at = 0
        for i in range(n_parts):
            own, other = parts[2 * i:2 * i + 2]
            n = own.shape[1]
            quarter = half // 2
            second, third = crossed(modes[i], own[quarter:], other[:quarter])
            hid_ref[:quarter, at:at + n] = own[:quarter]
            hid_ref[quarter:half, at:at + n] = second
            hid_ref[half:half + quarter, at:at + n] = third
            hid_ref[half + quarter:, at:at + n] = other[quarter:]
            at += n

    total = jnp.dot(hid_ref[...], w_ref[...], preferred_element_type=F32)
    if not first:
        total = total + acc_ref[...]
    if not last:
        refs[0][...] = total
        return
    keep_ref, send_ref, total_ref = refs[:3]
    total_ref[...] = total
    rows = half // 4
    for flip, ref, at in ((0, keep_ref, 0), (2, keep_ref, 2), (1, send_ref, 0), (3, send_ref, 2)):
        for part in range(2):
            v = total_ref[token_rows(flip, part, rows), :]
            ref[(at + part) * rows:(at + part + 1) * rows, :] = v.astype(ref.dtype)


def send_y_kernel(keep_ref, core_ref, o_ref):
    o_ref[...] = (keep_ref[...] + core_ref[...].astype(F32)).astype(BF16)


def final_kernel(keep_ref, core_ref, y_ref, o_ref):
    o_ref[...] = (keep_ref[...] + core_ref[...].astype(F32) + y_ref[...].astype(F32)).astype(BF16)


SHARES = (6, 6, 8, 6,)
SUM, GATHER = "mmmm", "nnmm"
GROUPS = ((0, 1,), (2,), (3,),)
ORDER = (
    "m0", "m1", "s", "a0", "q", "b0", "n", "m2", "a1", "m3", "c0", "b1",
    "a2", "d0", "c1", "b2", "a3", "e0", "d1", "c2", "b3", "e1", "d2", "c3",
    "w0", "e2", "d3", "e3", "w1", "w2",
)


def planned(tokens, norm_gain, gate_weight, up_weight, down_weight):
    rows, width = tokens.shape
    hidden = gate_weight.shape[1]
    out_width = down_weight.shape[1]
    unit = hidden // sum(SHARES)
    cuts = [unit * sum(SHARES[:k]) for k in range(len(SHARES) + 1)]
    gain = norm_gain[None, :]
    chain = Chain()

    t0 = tokens
    sq_shape = shape((rows, 128), F32)
    t2 = swap(t0, Y_SWAP)
    t1 = swap(t0, CORE_SWAP)
    (sq,) = chain.call(squares_kernel, [t0], [sq_shape], name="squares")
    squares = [sq, swap(sq, FIRST["m"])]
    (t2,) = chain.call(
        pass_kernel, [t2], [shape(t2.shape, BF16)], in_specs=[any_spec()], out_specs=[any_spec()], aliases={0: 0}, name="pass",
    )
    t3 = swap(t2, CORE_SWAP)
    (sq,) = chain.call(add_kernel, squares, [sq_shape], name="squares_add")
    squares = [sq, swap(sq, SECOND["m"])]
    (raw,) = chain.call(arrange_kernel, [t0, t1, t2, t3, gain], [shape((4 * rows, width), BF16)], name="arrange")

    state = [dict() for _ in SHARES]
    env = {"lhs": raw, "acc": None}

    def stage_s(k):
        (total,) = chain.call(add_kernel, squares, [sq_shape], name="squares_add")
        squares[:] = total, swap(total, THIRD)

    def stage_q(k):
        (s0,) = chain.call(add_kernel, squares, [sq_shape], name="squares_add")
        s2 = swap(s0, Y_SWAP)
        s1 = swap(s0, CORE_SWAP)
        env["s"] = (s0, s1, s2, swap(s0, BOTH_SWAP))

    def stage_n(k):
        env["lhs"], env["r"] = chain.call(
            functools.partial(norm_kernel, width * lax.axis_size("wa")),
            [t0, t1, t2, t3, *env["s"], gain],
            [shape((4 * rows, width), BF16), shape((4 * rows, 128), F32)],
            name="norm",
        )

    def stage_m(k):
        s = state[k]
        n = s["n"] = cuts[k + 1] - cuts[k]
        s["scaled"] = "r" not in env
        tile = 512 if n % 512 == 0 and cuts[k] % 512 == 0 else 256
        first = cuts[k] // tile
        s["keep"], send = chain.call(
            functools.partial(project_kernel, SUM[k]),
            [env["lhs"], gate_weight, up_weight],
            [shape((2, 2 * rows, n), F32), shape((2, 2 * rows, n), BF16)],
            grid=(n // tile,),
            in_specs=[
                pl.BlockSpec((4 * rows, width), lambda i: (0, 0)),
                pl.BlockSpec((width, tile), lambda i: (0, first + i)),
                pl.BlockSpec((width, tile), lambda i: (0, first + i)),
            ],
            out_specs=[pl.BlockSpec((2, 2 * rows, tile), lambda i: (0, 0, i))] * 2,
            flops=UNIT_FLOPS * 5 * SHARES[k],
            name="project",
        )
        s["parts"] = [swap(send, FIRST[SUM[k]])]

    def part(n, size, at):
        return pl.BlockSpec((2, size, n), lambda i: (0, at, 0))

    def add_up(k, size, pairs):
        s = state[k]
        n = s["n"]
        (send,) = chain.call(
            add_up_kernel, [s["keep"], *s["parts"]], [shape((2, size, n), BF16)],
            grid=(1,), in_specs=[part(n, size, 1)] * (1 + len(s["parts"])), out_specs=[part(n, size, 0)], name="add_up",
        )
        s["parts"].append(swap(send, pairs))

    def stage_a(k):
        add_up(k, rows, SECOND[SUM[k]])

    def stage_b(k):
        add_up(k, rows // 2, THIRD)

    def stage_c(k):
        s = state[k]
        n, size = s["n"], rows // 2
        (s["h"],) = chain.call(
            functools.partial(activate_kernel, s["scaled"]),
            [s["keep"], *s["parts"], env["r"]],
            [shape((size, n), BF16)],
            grid=(1,),
            in_specs=[part(n, size, 0)] * 4 + [pl.BlockSpec((size, 128), lambda i: (0, 0))],
            out_specs=[pl.BlockSpec((size, n), lambda i: (0, 0))],
            name="activate",
        )
        s["got"] = swap(s["h"], THIRD)

    def join(k, pairs):
        s = state[k]
        (s["h"],) = chain.call(
            join_kernel, [s["h"], s["got"]], [shape((2 * s["h"].shape[0], s["n"]), BF16)], name="join"
        )
        s["got"] = swap(s["h"], pairs)

    def stage_d(k):
        join(k, SECOND[GATHER[k]])

    def stage_e(k):
        join(k, FIRST[GATHER[k]])

    def stage_w(k):
        group = GROUPS[k]
        first, last = k == 0, k == len(GROUPS) - 1
        at, n = cuts[group[0]], cuts[group[-1] + 1] - cuts[group[0]]
        cols = 1024
        args, in_specs = [], []
        for j in group:
            args += [state[j]["h"], state[j]["got"]]
            in_specs += [pl.BlockSpec((2 * rows, state[j]["n"]), lambda i: (0, 0))] * 2
        args.append(down_weight)
        in_specs.append(pl.BlockSpec((pl.Element(n), pl.Element(cols)), lambda i: (at, i * cols)))
        if not first:
            args.append(env["acc"])
            in_specs.append(pl.BlockSpec((4 * rows, cols), lambda i: (0, i)))
        if last:
            out_shape = [shape((2 * rows, out_width), F32), shape((2 * rows, out_width), BF16)]
            out_specs = [pl.BlockSpec((2 * rows, cols), lambda i: (0, i))] * 2
            scratch = [pltpu.VMEM((4 * rows, cols), F32), pltpu.VMEM((4 * rows, n), BF16)]
        else:
            out_shape = [shape((4 * rows, out_width), F32)]
            out_specs = [pl.BlockSpec((4 * rows, cols), lambda i: (0, i))]
            scratch = [pltpu.VMEM((4 * rows, n), BF16)]
        env["last"] = chain.call(
            functools.partial(down_kernel, [GATHER[j] for j in group], first, last), args, out_shape,
            grid=(out_width // cols,), in_specs=in_specs, out_specs=out_specs, scratch=scratch,
            flops=UNIT_FLOPS * 2 * sum(SHARES[j] for j in group), name="down",
        )
        env["acc"] = env["last"][0]

    stages = dict(
        m=stage_m, a=stage_a, b=stage_b, c=stage_c, d=stage_d, e=stage_e, w=stage_w, s=stage_s, q=stage_q, n=stage_n
    )
    for step in ORDER:
        stages[step[0]](int(step[1:] or 0))

    keep, send = env["last"]
    core = swap(send, CORE_SWAP)
    block = lambda at: pl.BlockSpec((rows, out_width), lambda i: (at, 0))
    (send_y,) = chain.call(
        send_y_kernel, [keep, core], [shape((rows, out_width), BF16)],
        grid=(1,), in_specs=[block(1), block(1)], out_specs=[block(0)], name="send_y",
    )
    y = swap(send_y, Y_SWAP)
    (out,) = chain.call(
        final_kernel, [keep, core, y], [shape((rows, out_width), BF16)],
        grid=(1,), in_specs=[block(0)] * 3, out_specs=[block(0)], name="final",
    )
    return out


def general(tokens, norm_gain, gate_weight, up_weight, down_weight):
    gathered = lax.all_gather(tokens, "ha", axis=0, tiled=True).astype(F32)
    squares = lax.psum(jnp.sum(gathered * gathered, axis=1), "wa")
    mean_square = squares[:, None] / (gathered.shape[1] * lax.axis_size("wa"))
    normed = (gathered * lax.rsqrt(mean_square + EPS) * norm_gain[None, :]).astype(BF16)
    hidden = gate_weight.shape[1]
    gate = jnp.dot(normed, gate_weight, preferred_element_type=F32)
    up = jnp.dot(normed, up_weight, preferred_element_type=F32)
    summed = lax.psum_scatter(jnp.concatenate([gate, up], axis=1), "wa", scatter_dimension=0, tiled=True)
    mixed = (jax.nn.silu(summed[:, :hidden]) * summed[:, hidden:]).astype(BF16)
    out = jnp.dot(lax.all_gather(mixed, "wa", axis=0, tiled=True), down_weight, preferred_element_type=F32)
    return lax.psum_scatter(out, "ha", scatter_dimension=0, tiled=True).astype(BF16)


def solution(mesh):
    body = planned if (mesh.shape["wa"], mesh.shape["ha"]) == (8, 4) else general
    placed = (P("ha", "wa"), P("wa"), P("wa", "ha"), P("wa", "ha"), P("ha", "wa"))
    return jax.shard_map(body, mesh=mesh, in_specs=placed, out_specs=P("ha", "wa"), check_vma=False)
```
